32 devices in a mesh: gy: 8 (over y, x, core), pa: 4 (over z).
Axes of the slice: x: 2, y: 2, z: 4, core: 2. Of those that a mesh axis runs over, the one named last changes fastest.
Arguments:
- spectral_velocity: float32 [3, 16, 512, 1536], P(None, 'gy', 'pa'), may hold values from -0.01913664 to 0.01913664
- inverse_spacing: float32 [16], P('gy'), may hold values from 0.25 to 1
Outputs:
- increment: float32 [3, 16, 1152, 1536], P(None, 'gy', 'pa')
- vorticity_peak: float32 [], replicated
The draws below stay inside these ranges and needn't reach their ends.
All inputs are finite; a program needn't handle non-finite values.
Results may differ from the reference program's by a relative error of at most 0.00011.
Values sent between devices are 32-bit elements; how exact they have to be, the bound alone decides.
A program may use at most 128 MiB of HBM per device.

```python
import math
import jax
import jax.numpy as jnp
from jax import lax

NX = 1536
NZ = 1152
KX = 512
KZ = 768
NY = 16


def draw_spectral_velocity(key, part):
    key_values, key_planes = jax.random.split(key, 2)
    shape = (3, NY, KX, 2 * KZ)
    base = 0.5 / jnp.sqrt(jnp.float32(KX * KZ))
    planes = jnp.arange(NY, dtype=jnp.float32)
    rising = 1.0 + 2.0 * planes / max(NY - 1, 1)
    jitter = jnp.exp(jax.random.uniform(key_planes, (NY,), jnp.float32, jnp.log(0.7), jnp.log(1.4)))
    amplitude = (rising * jitter)[None, :, None, None]
    raw = jnp.clip(jax.random.normal(key_values, shape, jnp.float32), -4.0, 4.0)
    values = raw * base * amplitude
    return jnp.clip(values, -24.0 * base, 24.0 * base)


def shard_levels(key, shape, pieces, low, top_value):
    factor_of, own = 1.0, jax.random.fold_in(key, 6)
    for axis_at, shards_of in pieces:
        steps = jnp.exp(jax.random.uniform(jax.random.fold_in(own, axis_at), (shards_of,), jnp.float32, low / len(pieces), top_value / len(pieces)))
        factor_of = factor_of * jnp.repeat(steps, shape[axis_at] // shards_of).reshape([-1 if axis == axis_at else 1 for axis in range(len(shape))])
    return factor_of


def setup_inputs(seed: int = 0) -> dict:
    seeds = jax.random.split(jax.random.key(seed), 3)
    return {
        "spectral_velocity": draw_spectral_velocity(jax.random.fold_in(seeds[2], 71), 0),
        "inverse_spacing": jnp.clip(jnp.exp(math.log(1.0) - 1.3862944 * jax.random.uniform(seeds[1], (NY,), jnp.float32) ** shard_levels(seeds[1], (NY,), ((0, 8),), -0.2, 0.2)), 0.25, 1.0),
    }


def synthesize(modes):
    column = jnp.arange(KZ, dtype=jnp.int32)
    target = jnp.where(column < KZ // 2, column, column + (NZ - KZ))
    spread = jnp.zeros((modes.shape[0], KX, NZ), dtype=modes.dtype).at[:, :, target].set(modes)
    along_z = jnp.fft.ifft(spread, axis=-1) * NZ
    weight = jnp.where(jnp.arange(KX, dtype=jnp.int32) == 0, 1.0, 2.0)
    padded = jnp.zeros((modes.shape[0], NZ, NX), dtype=modes.dtype)
    padded = padded.at[:, :, :KX].set(jnp.transpose(along_z, (0, 2, 1)) * weight)
    return jnp.real(jnp.fft.ifft(padded, axis=-1) * NX)

def complexify(block):
    return block[..., :KZ] + 1j * block[..., KZ:]

def reference(spectral_velocity, inverse_spacing):
    wave_x = (jnp.arange(KX, dtype=jnp.int32).astype(jnp.float32) * (2.0 * math.pi / NX))[:, None]
    column = jnp.arange(KZ, dtype=jnp.int32)
    wave_z = jnp.where(column < KZ // 2, column, column - KZ).astype(jnp.float32) * (2.0 * math.pi / NZ)
    padded = jnp.pad(spectral_velocity, ((0, 0), (1, 1), (0, 0), (0, 0)))
    pair = jnp.array([0, 2], dtype=jnp.int32)

    def one_plane(index):
        below = complexify(lax.dynamic_index_in_dim(padded, index, 1, keepdims=False))
        center = complexify(lax.dynamic_index_in_dim(padded, index + 1, 1, keepdims=False))
        above = complexify(lax.dynamic_index_in_dim(padded, index + 2, 1, keepdims=False))
        spectra = jnp.stack((center[0], center[1], center[2], 1j * wave_z * center[1], 1j * wave_z * center[0] - 1j * wave_x * center[2], 1j * wave_x * center[1]))
        fields = synthesize(spectra)
        lower = synthesize(below[pair])
        upper = synthesize(above[pair])
        scale = lax.dynamic_index_in_dim(inverse_spacing, index, 0, keepdims=False)
        dy_u = (upper[0] - lower[0]) * scale
        dy_w = (upper[1] - lower[1]) * scale
        vort_x = dy_w - fields[3]
        vort_y = fields[4]
        vort_z = fields[5] - dy_u
        lamb = jnp.stack((fields[1] * vort_z - fields[2] * vort_y, fields[2] * vort_x - fields[0] * vort_z, fields[0] * vort_y - fields[1] * vort_x))
        return (lamb, jnp.max(vort_x * vort_x + vort_y * vort_y + vort_z * vort_z))
    lamb, peaks = lax.map(one_plane, jnp.arange(NY, dtype=jnp.int32))
    peak = jnp.sqrt(jnp.max(peaks))
    return (jnp.transpose(lamb, (1, 0, 2, 3)) / (peak + 1e-06), peak)
```

```python
import math

import numpy as np

import jax
import jax.numpy as jnp
from jax import lax
from jax.sharding import PartitionSpec as P

NX = 1536
NZ = 1152
KX = 512


def z_table(length, modes, parts):
    column = np.arange(modes)
    wave = np.where(column < modes // 2, column, column - modes)
    angles = (wave[None, :] * np.arange(length)[:, None] % length) * (2.0 * math.pi / length)
    cos, sin = np.cos(angles), np.sin(angles)
    scale = (wave * (2.0 * math.pi / length))[None, :]

    def lay(rr, ri, ir, ii):
        real = np.concatenate((rr, ri), 1).reshape(parts, 1, length // parts, 2 * modes)
        imag = np.concatenate((ir, ii), 1).reshape(parts, 1, length // parts, 2 * modes)
        both = np.concatenate((real, imag), 1)
        return both.reshape(parts, -1, 2 * modes).astype(np.float32)

    plain = lay(cos, -sin, sin, cos)
    slope = lay(-scale * sin, -scale * cos, scale * cos, -scale * sin)
    return plain, slope


def x_table(length, modes, parts):
    column = np.arange(modes)
    angles = (column[:, None] * np.arange(length)[None, :] % length) * (2.0 * math.pi / length)
    weight = np.where(column == 0, 1.0, 2.0)[:, None]
    both = np.stack((weight * np.cos(angles), -weight * np.sin(angles)))
    both = both.reshape(2, parts, modes // parts, length)
    return np.moveaxis(both, 1, 0).astype(np.float32)


def everywhere_max(value, axes):
    for axis in axes:
        count = lax.axis_size(axis)
        shift = 1
        while shift < count:
            pairs = [(i, (i + shift) % count) for i in range(count)]
            value = jnp.maximum(value, lax.ppermute(value, axis, pairs))
            shift *= 2
    return value


def body(spectral_velocity, inverse_spacing):
    planes, kx_local, width = spectral_velocity.shape[1:]
    parts = lax.axis_size("pa")
    levels = lax.axis_size("gy")
    me = lax.axis_index("pa")
    slab = NZ // parts
    plain, slope = z_table(NZ, width // 2, parts)
    order = (me - jnp.arange(parts)) % parts
    pieces = x_table(NX, KX, parts)
    pieces = np.concatenate([pieces[[-k % parts]] for k in range(2 * parts)])
    pieces = np.ascontiguousarray(np.moveaxis(pieces, 1, 0)).reshape(2, -1, NX)
    table_x = lax.dynamic_slice_in_dim(
        jnp.asarray(pieces), (parts - me) * kx_local, KX, axis=1
    ).reshape(2 * KX, NX)
    kx = (order[:, None] * kx_local + jnp.arange(kx_local)[None, :]).reshape(-1)
    wave_x = kx.astype(jnp.float32) * (2.0 * math.pi / NX)

    def exchange(modes, table):
        out = jnp.einsum(
            "dnk,fjmk->dfjnm", table, modes, precision=lax.Precision.HIGH,
            preferred_element_type=jnp.float32,
        )
        got = [lax.dynamic_index_in_dim(out, me, 0, keepdims=False)]
        for shift in range(1, parts):
            block = lax.dynamic_index_in_dim(out, (me + shift) % parts, 0, keepdims=False)
            got.append(lax.ppermute(block, "pa", [(i, (i + shift) % parts) for i in range(parts)]))
        whole = jnp.concatenate(got, axis=-1)
        return whole.reshape(whole.shape[:2] + (2, slab, KX))

    def to_x(hat):
        flat = jnp.concatenate((hat[..., 0, :, :], hat[..., 1, :, :]), axis=-1)
        return jnp.einsum(
            "...zm,mx->...zx", flat, table_x, precision=lax.Precision.HIGH,
            preferred_element_type=jnp.float32,
        )

    def turned(hat):
        return jnp.stack((-wave_x * hat[..., 1, :, :], wave_x * hat[..., 0, :, :]), axis=-3)

    u_modes, v_modes, w_modes = (spectral_velocity[c : c + 1] for c in range(3))
    uw_hat = exchange(jnp.concatenate((u_modes, w_modes)), plain)
    dzu_hat = exchange(u_modes, slope)[0]
    v_hat = exchange(v_modes, plain)[0]
    dzv_hat = exchange(v_modes, slope)[0]

    below = lax.ppermute(uw_hat[:, -1:], "gy", [(i, i + 1) for i in range(levels - 1)])
    above = lax.ppermute(uw_hat[:, :1], "gy", [(i + 1, i) for i in range(levels - 1)])
    spacing = inverse_spacing[None, :, None, None, None]
    lower = jnp.concatenate((below, uw_hat[:, :-1]), axis=1)
    upper = jnp.concatenate((uw_hat[:, 1:], above), axis=1)
    slope_y = (upper - lower) * spacing

    u, w = to_x(uw_hat[0]), to_x(uw_hat[1])
    vort_y = to_x(dzu_hat - turned(uw_hat[1]))
    v = to_x(v_hat)
    vort_z = to_x(turned(v_hat) - slope_y[0])
    vort_x = to_x(slope_y[1] - dzv_hat)
    lamb = jnp.stack(
        (v * vort_z - w * vort_y, w * vort_x - u * vort_z, u * vort_y - v * vort_x)
    )
    local_peak = jnp.max(vort_x * vort_x + vort_y * vort_y + vort_z * vort_z)
    magnitude = jnp.sqrt(everywhere_max(local_peak, ("gy", "pa")))
    return (lamb / (magnitude + 1e-06), magnitude)


def solution(mesh):
    placed = (P(None, "gy", "pa", None), P("gy"))
    return jax.shard_map(
        body,
        mesh=mesh,
        in_specs=placed,
        out_specs=(P(None, "gy", "pa", None), P()),
        check_vma=False,
    )
```

```python
import math

import numpy as np

import jax
import jax.numpy as jnp
from jax import lax
from jax.sharding import PartitionSpec as P

NX = 1536
NZ = 1152
KX = 512


def z_table(length, modes, parts):
    column = np.arange(modes)
    wave = np.where(column < modes // 2, column, column - modes)
    angles = (wave[None, :] * np.arange(length)[:, None] % length) * (2.0 * math.pi / length)
    cos, sin = np.cos(angles), np.sin(angles)
    scale = (wave * (2.0 * math.pi / length))[None, :]

    def lay(rr, ri, ir, ii):
        real = np.concatenate((rr, ri), 1).reshape(parts, 1, length // parts, 2 * modes)
        imag = np.concatenate((ir, ii), 1).reshape(parts, 1, length // parts, 2 * modes)
        both = np.concatenate((real, imag), 1)
        return both.reshape(parts, -1, 2 * modes).astype(np.float32)

    plain = lay(cos, -sin, sin, cos)
    slope = lay(-scale * sin, -scale * cos, scale * cos, -scale * sin)
    return plain, slope


def x_table(length, modes, parts):
    column = np.arange(modes)
    angles = (column[:, None] * np.arange(length)[None, :] % length) * (2.0 * math.pi / length)
    weight = np.where(column == 0, 1.0, 2.0)[:, None]
    both = np.stack((weight * np.cos(angles), -weight * np.sin(angles)))
    both = both.reshape(2, parts, modes // parts, length)
    return np.moveaxis(both, 1, 0).astype(np.float32)


def everywhere_max(value, axes):
    for axis in axes:
        count = lax.axis_size(axis)
        shift = 1
        while shift < count:
            pairs = [(i, (i + shift) % count) for i in range(count)]
            value = jnp.maximum(value, lax.ppermute(value, axis, pairs))
            shift *= 2
    return value


def body(spectral_velocity, inverse_spacing):
    planes, kx_local, width = spectral_velocity.shape[1:]
    parts = lax.axis_size("pa")
    levels = lax.axis_size("gy")
    me = lax.axis_index("pa")
    slab = NZ // parts
    plain, slope = z_table(NZ, width // 2, parts)
    relays = parts == 4
    low = me < 2
    inner = jnp.logical_and(me > 0, me < parts - 1)
    pieces = x_table(NX, KX, parts)
    if relays:
        order = jnp.stack((me, me ^ 1, jnp.where(low, 3, 0), jnp.where(low, 2, 1)))
        pieces = jnp.asarray(np.ascontiguousarray(np.moveaxis(pieces, 1, 0)).reshape(2, KX, NX))
        table_x = jnp.concatenate(
            [
                lax.dynamic_slice_in_dim(pieces, order[i] * kx_local, kx_local, axis=1)
                for i in range(parts)
            ],
            axis=1,
        ).reshape(2 * KX, NX)
    else:
        order = (me - jnp.arange(parts)) % parts
        pieces = np.concatenate([pieces[[-k % parts]] for k in range(2 * parts)])
        pieces = np.ascontiguousarray(np.moveaxis(pieces, 1, 0)).reshape(2, -1, NX)
        table_x = lax.dynamic_slice_in_dim(
            jnp.asarray(pieces), (parts - me) * kx_local, KX, axis=1
        ).reshape(2 * KX, NX)
    kx = (order[:, None] * kx_local + jnp.arange(kx_local)[None, :]).reshape(-1)
    wave_x = kx.astype(jnp.float32) * (2.0 * math.pi / NX)

    def exchange(modes, table):
        out = jnp.einsum(
            "dnk,fjmk->dfjnm", table, modes, precision=lax.Precision.HIGH,
            preferred_element_type=jnp.float32,
        )
        got = [lax.dynamic_index_in_dim(out, me, 0, keepdims=False)]
        for shift in range(1, parts):
            block = lax.dynamic_index_in_dim(out, (me + shift) % parts, 0, keepdims=False)
            got.append(lax.ppermute(block, "pa", [(i, (i + shift) % parts) for i in range(parts)]))
        whole = jnp.concatenate(got, axis=-1)
        return whole.reshape(whole.shape[:2] + (2, slab, KX))

    def pick(blocks, index):
        return lax.dynamic_index_in_dim(blocks, index, 0, keepdims=False)

    def product(table, modes, form):
        return jnp.einsum(
            form, table, modes, precision=lax.Precision.HIGH,
            preferred_element_type=jnp.float32,
        )

    def joined(blocks):
        whole = jnp.concatenate(blocks, axis=-1)
        return whole.reshape(whole.shape[:1] + (2, slab, KX))

    swap = [(i, i ^ 1) for i in range(parts)]

    def relayed(modes):
        raw = jnp.stack(
            (
                lax.ppermute(modes, "pa", [(0, 2), (3, 1)]),
                lax.ppermute(modes, "pa", [(1, 2), (2, 1)]),
            )
        )
        hats = []
        for table in (plain, slope):
            pair = lax.dynamic_slice_in_dim(jnp.asarray(table), (me // 2) * 2, 2, axis=0)
            near = product(pair, modes, "dnk,jmk->djnm")
            beside = lax.ppermute(pick(near, 1 - me % 2), "pa", swap)
            far = product(pair, raw, "dnk,sjmk->dsjnm")
            onward = lax.ppermute(pick(far, 1 - me % 2), "pa", [(1, 0), (2, 3)])
            far = jnp.where(inner, pick(far, me % 2), onward)
            hats.append(joined([pick(near, me % 2), beside, far[0], far[1]]))
        return hats

    def direct(modes):
        out = product(plain, modes, "dnk,jmk->djnm")
        got = [pick(out, me)]
        for bits in range(1, 4):
            got.append(
                lax.ppermute(pick(out, me ^ bits), "pa", [(i, i ^ bits) for i in range(parts)])
            )
        return joined(
            [got[0], got[1], jnp.where(inner, got[2], got[3]), jnp.where(inner, got[3], got[2])]
        )

    def to_x(hat):
        flat = jnp.concatenate((hat[..., 0, :, :], hat[..., 1, :, :]), axis=-1)
        return jnp.einsum(
            "...zm,mx->...zx", flat, table_x, precision=lax.Precision.HIGH,
            preferred_element_type=jnp.float32,
        )

    def turned(hat):
        return jnp.stack((-wave_x * hat[..., 1, :, :], wave_x * hat[..., 0, :, :]), axis=-3)

    def edges(hat):
        below = lax.ppermute(hat[-1:], "gy", [(i, i + 1) for i in range(levels - 1)])
        above = lax.ppermute(hat[:1], "gy", [(i + 1, i) for i in range(levels - 1)])
        lower = jnp.concatenate((below, hat[:-1]))
        upper = jnp.concatenate((hat[1:], above))
        return (upper - lower) * inverse_spacing[:, None, None, None]

    if relays:
        u_hat, dzu_hat = relayed(spectral_velocity[0])
        w_hat = direct(spectral_velocity[2])
        v_hat, dzv_hat = relayed(spectral_velocity[1])
    else:
        u_modes, v_modes, w_modes = (spectral_velocity[c : c + 1] for c in range(3))
        u_hat, w_hat = exchange(jnp.concatenate((u_modes, w_modes)), plain)
        dzu_hat = exchange(u_modes, slope)[0]
        v_hat = exchange(v_modes, plain)[0]
        dzv_hat = exchange(v_modes, slope)[0]

    u, w = to_x(u_hat), to_x(w_hat)
    vort_y = to_x(dzu_hat - turned(w_hat))
    v = to_x(v_hat)
    vort_z = to_x(turned(v_hat) - edges(u_hat))
    vort_x = to_x(edges(w_hat) - dzv_hat)
    lamb = jnp.stack(
        (v * vort_z - w * vort_y, w * vort_x - u * vort_z, u * vort_y - v * vort_x)
    )
    local_peak = jnp.max(vort_x * vort_x + vort_y * vort_y + vort_z * vort_z)
    magnitude = jnp.sqrt(everywhere_max(local_peak, ("gy", "pa")))
    return (lamb / (magnitude + 1e-06), magnitude)


def solution(mesh):
    placed = (P(None, "gy", "pa", None), P("gy"))
    return jax.shard_map(
        body,
        mesh=mesh,
        in_specs=placed,
        out_specs=(P(None, "gy", "pa", None), P()),
        check_vma=False,
    )
```

```python
import math

import numpy as np

import jax
import jax.numpy as jnp
from jax import lax
from jax.sharding import PartitionSpec as P

NX = 1536
NZ = 1152
KX = 512


def z_table(length, modes, parts):
    column = np.arange(modes)
    wave = np.where(column < modes // 2, column, column - modes)
    angles = (wave[None, :] * np.arange(length)[:, None] % length) * (2.0 * math.pi / length)
    cos, sin = np.cos(angles), np.sin(angles)
    scale = (wave * (2.0 * math.pi / length))[None, :]

    def lay(rr, ri, ir, ii):
        real = np.concatenate((rr, ri), 1).reshape(parts, 1, length // parts, 2 * modes)
        imag = np.concatenate((ir, ii), 1).reshape(parts, 1, length // parts, 2 * modes)
        both = np.concatenate((real, imag), 1)
        return both.reshape(parts, -1, 2 * modes).astype(np.float32)

    plain = lay(cos, -sin, sin, cos)
    slope = lay(-scale * sin, -scale * cos, scale * cos, -scale * sin)
    return plain, slope


def x_table(length, modes, parts):
    column = np.arange(modes)
    angles = (column[:, None] * np.arange(length)[None, :] % length) * (2.0 * math.pi / length)
    weight = np.where(column == 0, 1.0, 2.0)[:, None]
    both = np.stack((weight * np.cos(angles), -weight * np.sin(angles)))
    both = both.reshape(2, parts, modes // parts, length)
    return np.moveaxis(both, 1, 0).astype(np.float32)


def everywhere_max(value, axes):
    for axis in axes:
        count = lax.axis_size(axis)
        shift = 1
        while shift < count:
            pairs = [(i, (i + shift) % count) for i in range(count)]
            value = jnp.maximum(value, lax.ppermute(value, axis, pairs))
            shift *= 2
    return value


def body(spectral_velocity, inverse_spacing):
    planes, kx_local, width = spectral_velocity.shape[1:]
    parts = lax.axis_size("pa")
    levels = lax.axis_size("gy")
    me = lax.axis_index("pa")
    slab = NZ // parts
    plain, slope = z_table(NZ, width // 2, parts)
    order = (me - jnp.arange(parts)) % parts
    pieces = x_table(NX, KX, parts)
    pieces = np.concatenate([pieces[[-k % parts]] for k in range(2 * parts)])
    pieces = np.ascontiguousarray(np.moveaxis(pieces, 1, 0)).reshape(2, -1, NX)
    table_x = lax.dynamic_slice_in_dim(
        jnp.asarray(pieces), (parts - me) * kx_local, KX, axis=1
    ).reshape(2 * KX, NX)
    kx = (order[:, None] * kx_local + jnp.arange(kx_local)[None, :]).reshape(-1)
    wave_x = kx.astype(jnp.float32) * (2.0 * math.pi / NX)

    def synthesized(modes, table):
        out = jnp.einsum(
            "dnk,fjmk->dfjnm", table, modes, precision=lax.Precision.HIGH,
            preferred_element_type=jnp.float32,
        )
        return [
            lax.dynamic_index_in_dim(out, (me + shift) % parts, 0, keepdims=False)
            for shift in range(parts)
        ]

    def exchange(blocks):
        got = [blocks[0]]
        for shift in range(1, parts):
            pairs = [(i, (i + shift) % parts) for i in range(parts)]
            got.append(lax.ppermute(blocks[shift], "pa", pairs))
        whole = jnp.concatenate(got, axis=-1)
        return whole.reshape(whole.shape[:2] + (2, slab, KX)), got[1:]

    def to_x(hat):
        flat = jnp.concatenate((hat[..., 0, :, :], hat[..., 1, :, :]), axis=-1)
        return jnp.einsum(
            "...zm,mx->...zx", flat, table_x, precision=lax.Precision.HIGH,
            preferred_element_type=jnp.float32,
        )

    def turned(hat):
        return jnp.stack((-wave_x * hat[..., 1, :, :], wave_x * hat[..., 0, :, :]), axis=-3)

    def edges(hat):
        below = lax.ppermute(hat[:, -1:], "gy", [(i, i + 1) for i in range(levels - 1)])
        above = lax.ppermute(hat[:, :1], "gy", [(i + 1, i) for i in range(levels - 1)])
        lower = jnp.concatenate((below, hat[:, :-1]), axis=1)
        upper = jnp.concatenate((hat[:, 1:], above), axis=1)
        return (upper - lower) * inverse_spacing[None, :, None, None, None]

    u_modes, v_modes, w_modes = (spectral_velocity[c : c + 1] for c in range(3))
    first = synthesized(jnp.concatenate((u_modes, w_modes)), plain)
    pair_hat, got_pair = exchange(first)
    (u_late, v_late), _ = lax.optimization_barrier(((u_modes, v_modes), first))
    second = zip(synthesized(u_late, slope), synthesized(v_late, plain))
    second_hat, _ = exchange([jnp.concatenate(both) for both in second])
    last, _ = lax.optimization_barrier((synthesized(v_late, slope), got_pair))
    dzv_hat = exchange(last)[0][0]
    (u_hat, w_hat), (dzu_hat, v_hat) = pair_hat, second_hat
    slope_y = edges(pair_hat)

    u, w = to_x(u_hat), to_x(w_hat)
    vort_y = to_x(dzu_hat - turned(w_hat))
    v = to_x(v_hat)
    vort_z = to_x(turned(v_hat) - slope_y[0])
    vort_x = to_x(slope_y[1] - dzv_hat)
    lamb = jnp.stack(
        (v * vort_z - w * vort_y, w * vort_x - u * vort_z, u * vort_y - v * vort_x)
    )
    local_peak = jnp.max(vort_x * vort_x + vort_y * vort_y + vort_z * vort_z)
    magnitude = jnp.sqrt(everywhere_max(local_peak, ("gy", "pa")))
    return (lamb / (magnitude + 1e-06), magnitude)


def solution(mesh):
    placed = (P(None, "gy", "pa", None), P("gy"))
    return jax.shard_map(
        body,
        mesh=mesh,
        in_specs=placed,
        out_specs=(P(None, "gy", "pa", None), P()),
        check_vma=False,
    )
```
